128 devices in a mesh: outer: 16 (over z, y_lo, core), inner: 8 (over y_hi, x).
Axes of the slice: x: 4, y: 4 (y_hi: 2, y_lo: 2; y = y_hi * 2 + y_lo), z: 4, core: 2. Of those that a mesh axis runs over, the one named last changes fastest.
Arguments:
- query_in: bfloat16 [32768, 4096], P(('outer', 'inner')), may hold values from -12 to 12
- key_in: bfloat16 [32768, 1024], P(('outer', 'inner')), may hold values from -6 to 6
- value_in: bfloat16 [32768, 1024], P(('outer', 'inner')), may hold values from -6 to 6
- grad_out: bfloat16 [32768, 4096], P(('outer', 'inner')), may hold values from -6 to 6
- doc_ids: int32 [32768], P(('outer', 'inner')), may hold values from 0 to 127, never falling along the last dimension, each value on 1 to 1025 neighbouring positions
Outputs:
- query_grad: bfloat16 [32768, 4096], P(('outer', 'inner'))
- key_grad: bfloat16 [32768, 1024], P(('outer', 'inner'))
- value_grad: bfloat16 [32768, 1024], P(('outer', 'inner'))
The draws below stay inside these ranges and needn't reach their ends.
Inputs may be any that keep to these rules, and one draw needn't show every extreme that they name: doc_ids never fall along the sequence; a document holds at most 1025 tokens, and one holds exactly that many.
All inputs are finite; a program needn't handle non-finite values.
Results may differ from the reference program's by a relative error of at most 0.0078.
Values may be sent and summed in bfloat16 or wider, within the bound.
No kernel may reach another device: no remote copies, remote signals or barrier semaphores. Data moves between devices by JAX's collectives and lax.ppermute only.
A program may use at most 192 MiB of HBM per device.

```python
import math
import jax
import jax.numpy as jnp
import numpy as np
from jax import lax

H = 32
KVH = 8
DH = 128
T_DEV = 256
REACH = 4
TOKENS = 32768


def draw_key_in(key, part):
    key = jax.random.fold_in(key, 11)
    base = jnp.clip(jax.random.normal(key, (TOKENS, KVH * DH), jnp.float32), -6.0, 6.0)
    return base.astype(jnp.bfloat16)


def draw_query_in(key, part):
    key = jax.random.fold_in(key, 12)
    base = jnp.clip(jax.random.normal(key, (TOKENS, H * DH), jnp.float32), -6.0, 6.0)
    return base.astype(jnp.bfloat16)


def block_scale(key, shape, pieces, low, largest):
    def one(position, parts):
        heights = jax.random.uniform(jax.random.fold_in(jax.random.fold_in(key, 6), position), (parts,), jnp.float32, low / len(pieces), largest / len(pieces))
        return jnp.repeat(jnp.exp(heights), shape[position] // parts).reshape((-1,) + (1,) * (len(shape) - position - 1))

    loudness = one(*pieces[0])
    for cut in pieces[1:]:
        loudness = loudness * one(*cut)
    return loudness


def length_profile(count, total, limit, slope):
    loads = [(1 << 20) // math.isqrt(rank ** slope) + 1 for rank in range(2, count + 1)]
    rest, holding = total - limit - (count - 1), [1] * (count - 1)
    while rest > 0:
        movable = [i for i in range(count - 1) if holding[i] < limit]
        pool, remaining = sum([loads[i] for i in movable]), rest
        for i in movable:
            addition = min(limit - holding[i], max(1, remaining * loads[i] // pool), rest)
            holding[i] = holding[i] + addition
            rest = rest - addition
    return np.array([limit] + holding)


def ragged(rng, amount, total, bound, lean):
    if amount == 2:
        one = jax.random.randint(rng, (), max(1, total - bound), min(bound, total - 1) + 1)
        return jnp.stack([one, total - one])
    lengths = jnp.asarray(length_profile(amount, total, bound, lean), jnp.int32)
    couples = (amount - 1) // 2
    donor, receiver = lengths[1:1 + 2 * couples:2], lengths[2:2 + 2 * couples:2]
    margin = jnp.minimum(donor - 1, bound - receiver)
    passed = jax.random.randint(jax.random.fold_in(rng, 1), (couples,), 0, 1 << 20) % (margin + 1)
    lengths = lengths.at[1:1 + 2 * couples:2].set(donor - passed).at[2:2 + 2 * couples:2].set(receiver + passed)
    return lengths[jax.random.permutation(jax.random.fold_in(rng, 2), amount)]


def bell_draw(stream_key, extent, scale, most, cuts=(), kind=jnp.bfloat16):
    level = block_scale(stream_key, extent, cuts, -0.22, 0.18) if cuts else 1.0
    drawn = jax.random.normal(stream_key, extent, jnp.float32) * scale * level
    return jnp.minimum(jnp.maximum(drawn, -most), most).astype(kind)


def setup_inputs(seed: int = 0) -> dict:
    key_of = jax.random.split(jax.random.key(seed), 6)
    query_in = draw_query_in(jax.random.fold_in(key_of[5], 71), 0)
    key_in = draw_key_in(jax.random.fold_in(key_of[5], 71), 0)
    value_in = bell_draw(key_of[2], (TOKENS, KVH * DH), 1.0, 6.0, ((0, 128),))
    grad_out = bell_draw(key_of[3], (TOKENS, H * DH), 1.0, 6.0, ((0, 128),))
    doc_ids = jnp.searchsorted(jnp.cumsum(ragged(key_of[4], TOKENS // T_DEV, TOKENS, REACH * T_DEV + 1, 2)), jnp.arange(TOKENS), side="right").astype(jnp.int32)
    return {"query_in": query_in, "key_in": key_in, "value_in": value_in, "grad_out": grad_out, "doc_ids": doc_ids}


def reference(query_in, key_in, value_in, grad_out, doc_ids):
    key_span = REACH * T_DEV
    key_window = key_span + T_DEV
    group_size = H // KVH
    scaling = 1.0 / math.sqrt(DH)
    zero_rows = jnp.zeros((key_span, KVH * DH), jnp.bfloat16)
    key_pad = jnp.concatenate([zero_rows, key_in], axis=0)
    value_pad = jnp.concatenate([zero_rows, value_in], axis=0)
    doc_pad = jnp.concatenate([jnp.full((key_span,), -1, jnp.int32), doc_ids.astype(jnp.int32)], axis=0)
    pos_query = jnp.arange(T_DEV, dtype=jnp.int32)
    pos_key = jnp.arange(key_window, dtype=jnp.int32) - key_span

    def step(carry, block_index):
        key_acc, value_acc = carry
        block_start = (block_index * T_DEV).astype(jnp.int32)
        query_blk = lax.dynamic_slice_in_dim(query_in, block_start, T_DEV, 0).astype(jnp.float32).reshape(T_DEV, KVH, group_size, DH)
        grad_blk = lax.dynamic_slice_in_dim(grad_out, block_start, T_DEV, 0).astype(jnp.float32).reshape(T_DEV, KVH, group_size, DH)
        key_blk = lax.dynamic_slice_in_dim(key_pad, block_start, key_window, 0).astype(jnp.float32).reshape(key_window, KVH, DH)
        value_blk = lax.dynamic_slice_in_dim(value_pad, block_start, key_window, 0).astype(jnp.float32).reshape(key_window, KVH, DH)
        docs_query = lax.dynamic_slice_in_dim(doc_ids.astype(jnp.int32), block_start, T_DEV, 0)
        docs_key = lax.dynamic_slice_in_dim(doc_pad, block_start, key_window, 0)
        allowed = jnp.logical_and(docs_query[:, None] == docs_key[None, :], pos_key[None, :] <= pos_query[:, None])
        scores = jnp.einsum('tgcd,wgd->gctw', query_blk, key_blk) * scaling
        scores = jnp.where(allowed, scores, -1e+30)
        row_top = lax.optimization_barrier(jnp.max(scores, axis=-1, keepdims=True))
        weights = jnp.where(allowed, jnp.exp(scores - row_top), 0.0)
        prob = weights / lax.optimization_barrier(jnp.sum(weights, axis=-1, keepdims=True))
        prob_low = lax.optimization_barrier(prob.astype(jnp.bfloat16)).astype(jnp.float32)
        output = jnp.einsum('gctw,wgd->tgcd', prob_low, value_blk)
        delta = lax.optimization_barrier(jnp.sum(grad_blk * output, axis=-1))
        value_part = jnp.einsum('gctw,tgcd->wgd', prob_low, grad_blk)
        prob_grad = jnp.einsum('tgcd,wgd->gctw', grad_blk, value_blk)
        score_grad = prob * (prob_grad - jnp.transpose(delta, (1, 2, 0))[..., None])
        score_low = lax.optimization_barrier(score_grad.astype(jnp.bfloat16)).astype(jnp.float32)
        query_part = jnp.einsum('gctw,wgd->tgcd', score_low, key_blk) * scaling
        key_part = jnp.einsum('gctw,tgcd->wgd', score_low, query_blk) * scaling
        old_key = lax.dynamic_slice_in_dim(key_acc, block_start, key_window, 0)
        old_value = lax.dynamic_slice_in_dim(value_acc, block_start, key_window, 0)
        key_acc = lax.dynamic_update_slice_in_dim(key_acc, old_key + key_part.reshape(key_window, KVH * DH), block_start, 0)
        value_acc = lax.dynamic_update_slice_in_dim(value_acc, old_value + value_part.reshape(key_window, KVH * DH), block_start, 0)
        return ((key_acc, value_acc), query_part.reshape(T_DEV, H * DH).astype(jnp.bfloat16))
    start_acc = jnp.zeros((TOKENS + key_span, KVH * DH), jnp.float32)
    block_list = jnp.arange(TOKENS // T_DEV, dtype=jnp.int32)
    (key_acc, value_acc), query_parts = lax.scan(step, (start_acc, start_acc), block_list)
    query_grad = query_parts.reshape(TOKENS, H * DH)
    return (query_grad, key_acc[key_span:].astype(jnp.bfloat16), value_acc[key_span:].astype(jnp.bfloat16))
```

```python
import functools
import math

import jax
import jax.numpy as jnp
from jax import lax
from jax.experimental import pallas as pl
from jax.experimental.pallas import tpu as pltpu
from jax.sharding import PartitionSpec as P

H = 32
KVH = 8
DH = 128
REACH = 4
GROUP = H // KVH
ROW = 4
TAIL = 16
COST = 0
VMEM = 60 * 1024 * 1024
CHUNKS = (4, 4)
AXES = ("outer", "inner")
FAR = -1e30
FLOOR = -1e29
F32 = jnp.float32
BF16 = jnp.bfloat16


def ring(devices, step):
    return [(i, (i + step) % devices) for i in range(devices)]


def row_ring(devices, step):
    return [(i, i - i % ROW + (i + step) % ROW) for i in range(devices)]


def lead_kernel(tok, mark_ref, before_ref, q_ref, g_ref, k_ref, v_ref, b1_ref, b2_ref, b3_ref, b4_ref,
                dq_ref, own_ref, d1_ref, d2_ref, d3_ref, d4_ref, start_ref, *scratch):
    mark = mark_ref[...]
    same = jnp.zeros((TAIL, DH), F32)
    for ref in (b1_ref, b2_ref, b3_ref, b4_ref):
        same += (ref[0, tok:, :].astype(F32) == mark).astype(F32)
    reach = jnp.sum(same).astype(jnp.int32)
    before = before_ref[...]
    start = REACH * tok + jnp.where(before == 0, -reach, before)
    start_ref[...] = start
    attention(tok, start, q_ref, g_ref, k_ref, v_ref, b1_ref, b2_ref, b3_ref, b4_ref,
              dq_ref, own_ref, d1_ref, d2_ref, d3_ref, d4_ref, *scratch)


def follow_kernel(tok, start_ref, q_ref, g_ref, k_ref, v_ref, b1_ref, b2_ref, b3_ref, b4_ref,
                  dq_in_ref, *rest):
    attention(tok, start_ref[...], q_ref, g_ref, k_ref, v_ref, b1_ref, b2_ref, b3_ref, b4_ref,
              *rest)


def attention(tok, start, q_ref, g_ref, k_ref, v_ref, b1_ref, b2_ref, b3_ref, b4_ref,
              dq_ref, own_ref, d1_ref, d2_ref, d3_ref, d4_ref,
              kbuf, vbuf,
              kt, qt, gt, qs, gs, p_buf, dp_buf, top_buf, top, total, inner, dqt):
    scaling = 1.0 / math.sqrt(DH)
    to_exp2 = scaling * math.log2(math.e)
    far = REACH * tok
    live = jnp.clip(lax.div(far - jnp.min(start) + (tok - 1), tok), 0, REACH)
    behind = (b4_ref, b3_ref, b2_ref, b1_ref)
    for slot, ref in enumerate(behind):
        kbuf[slot * tok:(slot + 1) * tok, :] = ref[0, :tok, :]
        vbuf[slot * tok:(slot + 1) * tok, :] = ref[1, :tok, :]
    kbuf[far:, :] = k_ref[...]
    vbuf[far:, :] = v_ref[...]
    for slot in range(REACH + 1):
        kt[:, slot * tok:(slot + 1) * tok] = kbuf[slot * tok:(slot + 1) * tok, :].T
    for j in range(GROUP):
        rows, cols = slice(j * tok, (j + 1) * tok), slice(j * DH, (j + 1) * DH)
        qs[rows, :] = q_ref[:, cols]
        gs[rows, :] = g_ref[:, cols]
        qt[:, rows] = q_ref[:, cols].T
        gt[:, rows] = g_ref[:, cols].T
    row_id = lax.broadcasted_iota(jnp.int32, (tok, tok), 0)

    def first_pass(slot, own):
        base = slot * tok if own else pl.multiple_of(slot * tok, tok)
        keys = pl.ds(base, tok)
        k = kbuf[keys, :]
        v = vbuf[keys, :]
        allowed = row_id >= start - base
        if own:
            allowed = jnp.logical_and(allowed, row_id <= lax.broadcasted_iota(jnp.int32, (tok, tok), 1))
        raw = [jnp.dot(k, qt[:, j * tok:(j + 1) * tok], preferred_element_type=F32) for j in range(GROUP)]
        grads = [jnp.dot(v, gt[:, j * tok:(j + 1) * tok], preferred_element_type=F32) for j in range(GROUP)]
        for j in range(GROUP):
            cols = slice(j * tok, (j + 1) * tok)
            s = raw[j] * to_exp2
            dp = grads[j]
            s = jnp.where(allowed, s, FAR)
            high = jnp.max(s, axis=0, keepdims=True)
            if not own:
                old = top[:, cols]
                high = jnp.maximum(old, high)
                fade = jnp.exp2(old - high)
            p = jnp.exp2(s - high)
            p_sum = jnp.sum(p, axis=0, keepdims=True)
            dp_sum = jnp.sum(p * dp, axis=0, keepdims=True)
            if not own:
                p_sum = p_sum + total[:, cols] * fade
                dp_sum = dp_sum + inner[:, cols] * fade
            top[:, cols] = high
            top_buf[slot, :, cols] = high
            total[:, cols] = p_sum
            inner[:, cols] = dp_sum
            p_buf[keys, cols] = p
            dp_buf[keys, cols] = dp

    def second_pass(slot, own):
        base = slot * tok if own else pl.multiple_of(slot * tok, tok)
        keys = pl.ds(base, tok)
        ktile = kt[:, keys]
        lows, dss = [], []
        for j in range(GROUP):
            cols = slice(j * tok, (j + 1) * tok)
            weight = jnp.exp2(top_buf[slot, :, cols] - top[:, cols]) * total[:, cols]
            prob = p_buf[keys, cols] * weight
            lows.append(prob.astype(BF16))
            dss.append((prob * (dp_buf[keys, cols] - inner[:, cols])).astype(BF16))
        low = jnp.concatenate(lows, axis=1)
        ds = jnp.concatenate(dss, axis=1)
        dv = jnp.dot(low, gs[...], preferred_element_type=F32)
        dk = jnp.dot(ds, qs[...], preferred_element_type=F32)
        part = jnp.dot(ktile, ds, preferred_element_type=F32)
        if own:
            dqt[...] = part
        else:
            dqt[...] += part
        return dk * scaling, dv

    first_pass(REACH, True)

    def walk_first(i, carry):
        first_pass(REACH - 1 - i, False)
        return carry

    lax.fori_loop(0, live, walk_first, 0)
    share = 1.0 / total[...]
    inner[...] = inner[...] * share
    total[...] = share
    dk, dv = second_pass(REACH, True)
    own_ref[0] = dk
    own_ref[1] = dv
    for distance, ref in enumerate((d1_ref, d2_ref, d3_ref, d4_ref), start=1):
        @pl.when(live >= distance)
        def _():
            dk, dv = second_pass(REACH - distance, False)
            ref[0] = dk.astype(BF16)
            ref[1] = dv.astype(BF16)

        @pl.when(live < distance)
        def _():
            ref[...] = jnp.zeros_like(ref)

    for j in range(GROUP):
        dq_ref[:, j * DH:(j + 1) * DH] = (dqt[:, j * tok:(j + 1) * tok].T * scaling).astype(BF16)


def attend(first, heads, mark, start, query, grad, key, value, blocks, dq):
    tok = query.shape[0]
    lead = dq is None
    wide = GROUP * DH
    packed = pl.BlockSpec((2, tok, DH), lambda g, *_: (0, 0, g))
    block = pl.BlockSpec((2, blocks[0].shape[1], DH), lambda g, *_: (0, 0, g))
    big = pl.BlockSpec((tok, wide), lambda g, *_: (0, first + g))
    small = pl.BlockSpec((tok, DH), lambda g, *_: (0, first + g))
    vector = pl.BlockSpec((1, tok), lambda g, *_: (0, 0))
    window = (REACH + 1) * tok
    lanes = GROUP * tok
    pair = (2, tok, heads * DH)
    macs = heads * 5 * window * lanes * DH
    in_specs = [vector, big, big, small, small] + [block] * REACH
    out_specs = [big] + [packed] * (REACH + 1)
    out_shape = [jax.ShapeDtypeStruct(query.shape, BF16), jax.ShapeDtypeStruct(pair, F32)]
    out_shape += [jax.ShapeDtypeStruct(pair, BF16)] * REACH
    operands = [start, query, grad, key, value, *blocks]
    if lead:
        in_specs = [pl.BlockSpec((1, DH), lambda g, *_: (0, 0))] + in_specs
        operands = [mark] + operands
        out_specs += [vector]
        out_shape += [jax.ShapeDtypeStruct((1, tok), jnp.int32)]
    else:
        in_specs += [pl.BlockSpec(memory_space=pl.ANY)]
        operands += [dq]
    return pl.pallas_call(
        functools.partial(lead_kernel if lead else follow_kernel, tok),
        grid=(heads,),
        in_specs=in_specs,
        out_specs=out_specs,
        scratch_shapes=[
            pltpu.VMEM((window, DH), BF16),
            pltpu.VMEM((window, DH), BF16),
            pltpu.VMEM((DH, window), BF16),
            pltpu.VMEM((DH, lanes), BF16),
            pltpu.VMEM((DH, lanes), BF16),
            pltpu.VMEM((lanes, DH), BF16),
            pltpu.VMEM((lanes, DH), BF16),
            pltpu.VMEM((window, lanes), F32),
            pltpu.VMEM((window, lanes), F32),
            pltpu.VMEM((REACH + 1, 1, lanes), F32),
            pltpu.VMEM((1, lanes), F32),
            pltpu.VMEM((1, lanes), F32),
            pltpu.VMEM((1, lanes), F32),
            pltpu.VMEM((DH, lanes), F32),
        ],
        out_shape=out_shape,
        input_output_aliases={} if lead else {len(operands) - 1: 0},
        compiler_params=pltpu.CompilerParams(vmem_limit_bytes=VMEM),
        cost_estimate=pl.CostEstimate(flops=COST * macs, bytes_accessed=0, transcendentals=0),
    )(*operands)


def on_device(query_in, key_in, value_in, grad_out, doc_ids):
    tok = query_in.shape[0]
    devices = lax.axis_size(AXES)
    column = lax.axis_index("inner") % ROW

    def send(block, route):
        return lax.ppermute(block, AXES, route)

    marks = (doc_ids + 1).astype(BF16)
    spans = []
    first = 0
    for heads in CHUNKS:
        spans.append((first, heads))
        first += heads

    packs = []
    for first, heads in spans:
        cols = slice(first * DH, (first + heads) * DH)
        pack = jnp.stack([key_in[:, cols], value_in[:, cols]])
        if first == 0:
            tail = jnp.pad(marks.reshape(-1, DH), ((0, TAIL - tok // DH), (0, 0)))
            tail = jnp.broadcast_to(jnp.tile(tail, (1, heads))[None], (2, TAIL, heads * DH))
            pack = jnp.concatenate([pack, tail], axis=1)
        packs.append(pack)

    far = []
    operands = []
    for i, pack in enumerate(packs):
        if i > 0:
            pack, far[-1] = lax.optimization_barrier((pack, far[-1]))
        b4 = send(pack, ring(devices, REACH))
        far.append(b4)
        operands.append((jnp.where(column == ROW - 1, b4, pack), jnp.where(column < 2, pack, b4),
                         jnp.where(column == 0, pack, b4)))

    def exchange(i):
        one, two, three = operands[i]
        return (send(one, row_ring(devices, 1)), send(two, row_ring(devices, 2)),
                send(three, row_ring(devices, -1)), far[i])

    def give_back(sums):
        own, d1, d2, d3, d4 = sums
        g1 = send(d1, row_ring(devices, -1)).astype(F32)
        g2 = send(d2, row_ring(devices, 2)).astype(F32)
        g3 = send(d3, row_ring(devices, 1)).astype(F32)
        zero = jnp.zeros((), F32)
        e4 = (d4.astype(F32) + jnp.where(column == ROW - 1, g1, zero)
              + jnp.where(column >= 1, g3, zero) + jnp.where(column >= 2, g2, zero)).astype(BF16)
        mine = (own + jnp.where(column < ROW - 1, g1, zero) + jnp.where(column == 0, g3, zero)
                + jnp.where(column < 2, g2, zero))
        return e4, mine

    start = jnp.sum((doc_ids[:, None] < doc_ids[None, :]).astype(jnp.int32), axis=0)[None]
    mark = jnp.broadcast_to(marks[:1].astype(F32), (1, DH))
    query_grad = None
    returned = []
    blocks = exchange(0)
    for i, (first, heads) in enumerate(spans):
        if i + 1 < len(spans):
            blocks, operands[i + 1] = lax.optimization_barrier((blocks, operands[i + 1]))
            later = exchange(i + 1)
        query_grad, *sums = attend(first, heads, mark, start, query_in, grad_out, key_in,
                                   value_in, blocks, query_grad)
        if first == 0:
            *sums, start = sums
        if i + 1 < len(spans):
            blocks = later
            sums, blocks = lax.optimization_barrier((sums, blocks))
        if i > 0:
            sums, returned[-1] = lax.optimization_barrier((sums, returned[-1]))
        returned.append(give_back(sums))

    results = []
    for e4, mine in returned:
        results.append((mine + send(e4, ring(devices, -REACH)).astype(F32)).astype(BF16))
    key_grad = jnp.concatenate([r[0] for r in results], axis=1)
    value_grad = jnp.concatenate([r[1] for r in results], axis=1)
    return query_grad, key_grad, value_grad


def solution(mesh):
    rows = P(AXES, None)
    return jax.shard_map(
        on_device,
        mesh=mesh,
        in_specs=(rows, rows, rows, rows, P(AXES)),
        out_specs=(rows, rows, rows),
        check_vma=False,
    )
```

```python
import functools
import math

import jax
import jax.numpy as jnp
from jax import lax
from jax.experimental import pallas as pl
from jax.experimental.pallas import tpu as pltpu
from jax.sharding import PartitionSpec as P

H = 32
KVH = 8
DH = 128
REACH = 4
GROUP = H // KVH
ROW = 4
TAIL = 16
COST = 0
VMEM = 60 * 1024 * 1024
SENT = ((0, 3), (3, 5))
CALLS = ((0, 3, 0, 0), (3, 3, 1, 0), (6, 2, 1, 3))
BACK = ((0,), (1,), (2,))
AXES = ("outer", "inner")
FAR = -1e30
FLOOR = -1e29
F32 = jnp.float32
BF16 = jnp.bfloat16


def ring(devices, step):
    return [(i, (i + step) % devices) for i in range(devices)]


def row_ring(devices, step):
    return [(i, i - i % ROW + (i + step) % ROW) for i in range(devices)]


def lead_kernel(tok, mark_ref, before_ref, q_ref, g_ref, k_ref, v_ref, b1_ref, b2_ref, b3_ref, b4_ref,
                dq_ref, own_ref, d1_ref, d2_ref, d3_ref, d4_ref, start_ref, *scratch):
    mark = mark_ref[...]
    same = jnp.zeros((TAIL, DH), F32)
    for ref in (b1_ref, b2_ref, b3_ref, b4_ref):
        same += (ref[0, tok:, :].astype(F32) == mark).astype(F32)
    reach = jnp.sum(same).astype(jnp.int32)
    before = before_ref[...]
    start = REACH * tok + jnp.where(before == 0, -reach, before)
    start_ref[...] = start
    attention(tok, start, q_ref, g_ref, k_ref, v_ref, b1_ref, b2_ref, b3_ref, b4_ref,
              dq_ref, own_ref, d1_ref, d2_ref, d3_ref, d4_ref, *scratch)


def follow_kernel(tok, filled, start_ref, q_ref, g_ref, k_ref, v_ref, b1_ref, b2_ref, b3_ref, b4_ref, *rest):
    attention(tok, start_ref[...], q_ref, g_ref, k_ref, v_ref, b1_ref, b2_ref, b3_ref, b4_ref,
              *rest[filled:])


def attention(tok, start, q_ref, g_ref, k_ref, v_ref, b1_ref, b2_ref, b3_ref, b4_ref,
              dq_ref, own_ref, d1_ref, d2_ref, d3_ref, d4_ref,
              kbuf, vbuf,
              kt, qt, gt, qs, gs, p_buf, dp_buf, top_buf, top, total, inner, dqt):
    scaling = 1.0 / math.sqrt(DH)
    to_exp2 = scaling * math.log2(math.e)
    far = REACH * tok
    live = jnp.clip(lax.div(far - jnp.min(start) + (tok - 1), tok), 0, REACH)
    behind = (b4_ref, b3_ref, b2_ref, b1_ref)
    for slot, ref in enumerate(behind):
        kbuf[slot * tok:(slot + 1) * tok, :] = ref[0, :tok, :]
        vbuf[slot * tok:(slot + 1) * tok, :] = ref[1, :tok, :]
    kbuf[far:, :] = k_ref[...]
    vbuf[far:, :] = v_ref[...]
    for slot in range(REACH + 1):
        kt[:, slot * tok:(slot + 1) * tok] = kbuf[slot * tok:(slot + 1) * tok, :].T
    for j in range(GROUP):
        rows, cols = slice(j * tok, (j + 1) * tok), slice(j * DH, (j + 1) * DH)
        qs[rows, :] = q_ref[:, cols]
        gs[rows, :] = g_ref[:, cols]
        qt[:, rows] = q_ref[:, cols].T
        gt[:, rows] = g_ref[:, cols].T
    row_id = lax.broadcasted_iota(jnp.int32, (tok, tok), 0)

    def first_pass(slot, own):
        base = slot * tok if own else pl.multiple_of(slot * tok, tok)
        keys = pl.ds(base, tok)
        k = kbuf[keys, :]
        v = vbuf[keys, :]
        allowed = row_id >= start - base
        if own:
            allowed = jnp.logical_and(allowed, row_id <= lax.broadcasted_iota(jnp.int32, (tok, tok), 1))
        raw = [jnp.dot(k, qt[:, j * tok:(j + 1) * tok], preferred_element_type=F32) for j in range(GROUP)]
        grads = [jnp.dot(v, gt[:, j * tok:(j + 1) * tok], preferred_element_type=F32) for j in range(GROUP)]
        for j in range(GROUP):
            cols = slice(j * tok, (j + 1) * tok)
            s = raw[j] * to_exp2
            dp = grads[j]
            s = jnp.where(allowed, s, FAR)
            high = jnp.max(s, axis=0, keepdims=True)
            if not own:
                old = top[:, cols]
                high = jnp.maximum(old, high)
                fade = jnp.exp2(old - high)
            p = jnp.exp2(s - high)
            p_sum = jnp.sum(p, axis=0, keepdims=True)
            dp_sum = jnp.sum(p * dp, axis=0, keepdims=True)
            if not own:
                p_sum = p_sum + total[:, cols] * fade
                dp_sum = dp_sum + inner[:, cols] * fade
            top[:, cols] = high
            top_buf[slot, :, cols] = high
            total[:, cols] = p_sum
            inner[:, cols] = dp_sum
            p_buf[keys, cols] = p
            dp_buf[keys, cols] = dp

    def second_pass(slot, own):
        base = slot * tok if own else pl.multiple_of(slot * tok, tok)
        keys = pl.ds(base, tok)
        ktile = kt[:, keys]
        lows, dss = [], []
        for j in range(GROUP):
            cols = slice(j * tok, (j + 1) * tok)
            weight = jnp.exp2(top_buf[slot, :, cols] - top[:, cols]) * total[:, cols]
            prob = p_buf[keys, cols] * weight
            lows.append(prob.astype(BF16))
            dss.append((prob * (dp_buf[keys, cols] - inner[:, cols])).astype(BF16))
        low = jnp.concatenate(lows, axis=1)
        ds = jnp.concatenate(dss, axis=1)
        dv = jnp.dot(low, gs[...], preferred_element_type=F32)
        dk = jnp.dot(ds, qs[...], preferred_element_type=F32)
        part = jnp.dot(ktile, ds, preferred_element_type=F32)
        if own:
            dqt[...] = part
        else:
            dqt[...] += part
        return dk * scaling, dv

    first_pass(REACH, True)

    def walk_first(i, carry):
        first_pass(REACH - 1 - i, False)
        return carry

    lax.fori_loop(0, live, walk_first, 0)
    share = 1.0 / total[...]
    inner[...] = inner[...] * share
    total[...] = share
    dk, dv = second_pass(REACH, True)
    own_ref[0] = dk
    own_ref[1] = dv
    for distance, ref in enumerate((d1_ref, d2_ref, d3_ref, d4_ref), start=1):
        @pl.when(live >= distance)
        def _():
            dk, dv = second_pass(REACH - distance, False)
            ref[0] = dk.astype(BF16)
            ref[1] = dv.astype(BF16)

        @pl.when(live < distance)
        def _():
            ref[...] = jnp.zeros_like(ref)

    for j in range(GROUP):
        dq_ref[:, j * DH:(j + 1) * DH] = (dqt[:, j * tok:(j + 1) * tok].T * scaling).astype(BF16)


def attend(first, heads, place, at, width, mark, start, query, grad, key, value, blocks, filled):
    tok = query.shape[0]
    lead = not filled
    wide = GROUP * DH
    packed = pl.BlockSpec((2, tok, DH), lambda g: (0, 0, at + g))
    block = pl.BlockSpec((2, blocks[0].shape[1], DH), lambda g: (0, 0, place + g))
    big = pl.BlockSpec((tok, wide), lambda g: (0, first + g))
    small = pl.BlockSpec((tok, DH), lambda g: (0, first + g))
    vector = pl.BlockSpec((1, tok), lambda g: (0, 0))
    window = (REACH + 1) * tok
    lanes = GROUP * tok
    pair = (2, tok, width * DH)
    macs = heads * 5 * window * lanes * DH
    in_specs = [vector, big, big, small, small] + [block] * REACH
    out_specs = [big] + [packed] * (REACH + 1)
    out_shape = [jax.ShapeDtypeStruct(query.shape, BF16), jax.ShapeDtypeStruct(pair, F32)]
    out_shape += [jax.ShapeDtypeStruct(pair, BF16)] * REACH
    operands = [start, query, grad, key, value, *blocks]
    aliases = {}
    if lead:
        kernel = functools.partial(lead_kernel, tok)
        in_specs = [pl.BlockSpec((1, DH), lambda g: (0, 0))] + in_specs
        operands = [mark] + operands
        out_specs += [vector]
        out_shape += [jax.ShapeDtypeStruct((1, tok), jnp.int32)]
    else:
        kernel = functools.partial(follow_kernel, tok, len(filled))
        aliases = {len(operands) + n: n for n in range(len(filled))}
        in_specs += [pl.BlockSpec(memory_space=pl.ANY)] * len(filled)
        operands += filled
    return pl.pallas_call(
        kernel,
        grid=(heads,),
        in_specs=in_specs,
        out_specs=out_specs,
        scratch_shapes=[
            pltpu.VMEM((window, DH), BF16),
            pltpu.VMEM((window, DH), BF16),
            pltpu.VMEM((DH, window), BF16),
            pltpu.VMEM((DH, lanes), BF16),
            pltpu.VMEM((DH, lanes), BF16),
            pltpu.VMEM((lanes, DH), BF16),
            pltpu.VMEM((lanes, DH), BF16),
            pltpu.VMEM((window, lanes), F32),
            pltpu.VMEM((window, lanes), F32),
            pltpu.VMEM((REACH + 1, 1, lanes), F32),
            pltpu.VMEM((1, lanes), F32),
            pltpu.VMEM((1, lanes), F32),
            pltpu.VMEM((1, lanes), F32),
            pltpu.VMEM((DH, lanes), F32),
        ],
        out_shape=out_shape,
        input_output_aliases=aliases,
        compiler_params=pltpu.CompilerParams(vmem_limit_bytes=VMEM),
        cost_estimate=pl.CostEstimate(flops=COST * macs, bytes_accessed=0, transcendentals=0),
    )(*operands)


def on_device(query_in, key_in, value_in, grad_out, doc_ids):
    tok = query_in.shape[0]
    devices = lax.axis_size(AXES)
    column = lax.axis_index("inner") % ROW

    def send(block, route):
        return lax.ppermute(block, AXES, route)

    marks = (doc_ids + 1).astype(BF16)
    packs = []
    for first, heads in SENT:
        cols = slice(first * DH, (first + heads) * DH)
        pack = jnp.stack([key_in[:, cols], value_in[:, cols]])
        if first == 0:
            tail = jnp.pad(marks.reshape(-1, DH), ((0, TAIL - tok // DH), (0, 0)))
            tail = jnp.broadcast_to(jnp.tile(tail, (1, heads))[None], (2, TAIL, heads * DH))
            pack = jnp.concatenate([pack, tail], axis=1)
        packs.append(pack)

    mark = jnp.broadcast_to(marks[:1].astype(F32), (1, DH))
    far = []
    operands = []
    for i, pack in enumerate(packs):
        if i > 0:
            pack, far[-1], mark = lax.optimization_barrier((pack, far[-1], mark))
        b4 = send(pack, ring(devices, REACH))
        far.append(b4)
        operands.append((jnp.where(column == ROW - 1, b4, pack), jnp.where(column < 2, pack, b4),
                         jnp.where(column == 0, pack, b4)))

    def exchange(i):
        one, two, three = operands[i]
        return (send(one, row_ring(devices, 1)), send(two, row_ring(devices, 2)),
                send(three, row_ring(devices, -1)), far[i])

    def give_back(sums):
        return send(sums[1], row_ring(devices, -1)), send(sums[2], row_ring(devices, 2)), send(sums[3], row_ring(devices, 1))

    def add_up(sums, given):
        own, d4 = sums[0], sums[4]
        g1, g2, g3 = (g.astype(F32) for g in given)
        zero = jnp.zeros((), F32)
        e4 = (d4.astype(F32) + jnp.where(column == ROW - 1, g1, zero)
              + jnp.where(column >= 1, g3, zero) + jnp.where(column >= 2, g2, zero)).astype(BF16)
        mine = (own + jnp.where(column < ROW - 1, g1, zero) + jnp.where(column == 0, g3, zero)
                + jnp.where(column < 2, g2, zero))
        return e4, mine

    start = jnp.sum((doc_ids[:, None] < doc_ids[None, :]).astype(jnp.int32), axis=0)[None]
    blocks = [exchange(0)]
    for i in range(1, len(SENT)):
        blocks[-1], operands[i] = lax.optimization_barrier((blocks[-1], operands[i]))
        blocks.append(exchange(i))
    query_grad = None
    returned = []
    given = None
    for group in BACK:
        width = sum(CALLS[call][1] for call in group)
        at = 0
        sums = []
        for call in group:
            first, heads, sent, place = CALLS[call]
            filled = [] if query_grad is None else [query_grad, *sums]
            query_grad, *sums = attend(first, heads, place, at, width, mark, start, query_in, grad_out,
                                       key_in, value_in, blocks[sent], filled)
            if not filled:
                *sums, start = sums
            at += heads
        if given is None:
            sums, blocks[-1] = lax.optimization_barrier((sums, blocks[-1]))
        else:
            sums, given = lax.optimization_barrier((sums, given))
            returned.append(add_up(before_sums, given))
        given = give_back(sums)
        before_sums = sums

    returned.append(add_up(before_sums, given))

    results = []
    for e4, mine in returned:
        results.append((mine + send(e4, ring(devices, -REACH)).astype(F32)).astype(BF16))
    key_grad = jnp.concatenate([r[0] for r in results], axis=1)
    value_grad = jnp.concatenate([r[1] for r in results], axis=1)
    return query_grad, key_grad, value_grad


def solution(mesh):
    rows = P(AXES, None)
    return jax.shard_map(
        on_device,
        mesh=mesh,
        in_specs=(rows, rows, rows, rows, P(AXES)),
        out_specs=(rows, rows, rows),
        check_vma=False,
    )
```

```python
import functools
import math

import jax
import jax.numpy as jnp
from jax import lax
from jax.experimental import pallas as pl
from jax.experimental.pallas import tpu as pltpu
from jax.sharding import PartitionSpec as P

H = 32
KVH = 8
DH = 128
REACH = 4
GROUP = H // KVH
ROW = 4
TAIL = 16
COST = 0
VMEM = 60 * 1024 * 1024
SENT = ((0, 3), (3, 5))
CALLS = ((0, 3, 0, 0), (3, 3, 1, 0), (6, 2, 1, 3))
BACK = ((0,), (1,), (2,))
AXES = ("outer", "inner")
FAR = -1e30
FLOOR = -1e29
F32 = jnp.float32
BF16 = jnp.bfloat16


def ring(devices, step):
    return [(i, (i + step) % devices) for i in range(devices)]


def row_ring(devices, step):
    return [(i, i - i % ROW + (i + step) % ROW) for i in range(devices)]


def lead_kernel(tok, mark_ref, before_ref, q_ref, g_ref, k_ref, v_ref, b1_ref, b2_ref, b3_ref, b4_ref,
                dq_ref, own_ref, d1_ref, d2_ref, d3_ref, d4_ref, start_ref, *scratch):
    mark = mark_ref[...]
    same = jnp.zeros((TAIL, DH), F32)
    for ref in (b1_ref, b2_ref, b3_ref, b4_ref):
        same += (ref[0, tok:, :].astype(F32) == mark).astype(F32)
    reach = jnp.sum(same).astype(jnp.int32)
    before = before_ref[...]
    start = REACH * tok + jnp.where(before == 0, -reach, before)
    start_ref[...] = start
    attention(tok, start, q_ref, g_ref, k_ref, v_ref, b1_ref, b2_ref, b3_ref, b4_ref,
              dq_ref, own_ref, d1_ref, d2_ref, d3_ref, d4_ref, *scratch)


def follow_kernel(tok, filled, start_ref, q_ref, g_ref, k_ref, v_ref, b1_ref, b2_ref, b3_ref, b4_ref, *rest):
    attention(tok, start_ref[...], q_ref, g_ref, k_ref, v_ref, b1_ref, b2_ref, b3_ref, b4_ref,
              *rest[filled:])


def attention(tok, start, q_ref, g_ref, k_ref, v_ref, b1_ref, b2_ref, b3_ref, b4_ref,
              dq_ref, own_ref, d1_ref, d2_ref, d3_ref, d4_ref,
              kbuf, vbuf,
              kt, qt, gt, qs, gs, p_buf, dp_buf, top_buf, top, total, inner, dqt):
    scaling = 1.0 / math.sqrt(DH)
    to_exp2 = scaling * math.log2(math.e)
    far = REACH * tok
    live = jnp.clip(lax.div(far - jnp.min(start) + (tok - 1), tok), 0, REACH)
    behind = (b4_ref, b3_ref, b2_ref, b1_ref)
    for slot, ref in enumerate(behind):
        kbuf[slot * tok:(slot + 1) * tok, :] = ref[0, :tok, :]
        vbuf[slot * tok:(slot + 1) * tok, :] = ref[1, :tok, :]
    kbuf[far:, :] = k_ref[...]
    vbuf[far:, :] = v_ref[...]
    for slot in range(REACH + 1):
        kt[:, slot * tok:(slot + 1) * tok] = kbuf[slot * tok:(slot + 1) * tok, :].T
    for j in range(GROUP):
        rows, cols = slice(j * tok, (j + 1) * tok), slice(j * DH, (j + 1) * DH)
        qs[rows, :] = q_ref[:, cols]
        gs[rows, :] = g_ref[:, cols]
        qt[:, rows] = q_ref[:, cols].T
        gt[:, rows] = g_ref[:, cols].T
    row_id = lax.broadcasted_iota(jnp.int32, (tok, tok), 0)

    def first_pass(slot, own):
        base = slot * tok if own else pl.multiple_of(slot * tok, tok)
        keys = pl.ds(base, tok)
        k = kbuf[keys, :]
        v = vbuf[keys, :]
        allowed = row_id >= start - base
        if own:
            allowed = jnp.logical_and(allowed, row_id <= lax.broadcasted_iota(jnp.int32, (tok, tok), 1))
        raw = [jnp.dot(k, qt[:, j * tok:(j + 1) * tok], preferred_element_type=F32) for j in range(GROUP)]
        grads = [jnp.dot(v, gt[:, j * tok:(j + 1) * tok], preferred_element_type=F32) for j in range(GROUP)]
        for j in range(GROUP):
            cols = slice(j * tok, (j + 1) * tok)
            s = raw[j] * to_exp2
            dp = grads[j]
            s = jnp.where(allowed, s, FAR)
            high = jnp.max(s, axis=0, keepdims=True)
            if not own:
                old = top[:, cols]
                high = jnp.maximum(old, high)
                fade = jnp.exp2(old - high)
            p = jnp.exp2(s - high)
            p_sum = jnp.sum(p, axis=0, keepdims=True)
            dp_sum = jnp.sum(p * dp, axis=0, keepdims=True)
            if not own:
                p_sum = p_sum + total[:, cols] * fade
                dp_sum = dp_sum + inner[:, cols] * fade
            top[:, cols] = high
            top_buf[slot, :, cols] = high
            total[:, cols] = p_sum
            inner[:, cols] = dp_sum
            p_buf[keys, cols] = p
            dp_buf[keys, cols] = dp

    def second_pass(slot, own):
        base = slot * tok if own else pl.multiple_of(slot * tok, tok)
        keys = pl.ds(base, tok)
        ktile = kt[:, keys]
        lows, dss = [], []
        for j in range(GROUP):
            cols = slice(j * tok, (j + 1) * tok)
            weight = jnp.exp2(top_buf[slot, :, cols] - top[:, cols]) * total[:, cols]
            prob = p_buf[keys, cols] * weight
            lows.append(prob.astype(BF16))
            dss.append((prob * (dp_buf[keys, cols] - inner[:, cols])).astype(BF16))
        low = jnp.concatenate(lows, axis=1)
        ds = jnp.concatenate(dss, axis=1)
        dv = jnp.dot(low, gs[...], preferred_element_type=F32)
        dk = jnp.dot(ds, qs[...], preferred_element_type=F32)
        part = jnp.dot(ktile, ds, preferred_element_type=F32)
        if own:
            dqt[...] = part
        else:
            dqt[...] += part
        return dk * scaling, dv

    first_pass(REACH, True)

    def walk_first(i, carry):
        first_pass(REACH - 1 - i, False)
        return carry

    lax.fori_loop(0, live, walk_first, 0)
    share = 1.0 / total[...]
    inner[...] = inner[...] * share
    total[...] = share
    dk, dv = second_pass(REACH, True)
    own_ref[0] = dk
    own_ref[1] = dv
    for distance, ref in enumerate((d1_ref, d2_ref, d3_ref, d4_ref), start=1):
        @pl.when(live >= distance)
        def _():
            dk, dv = second_pass(REACH - distance, False)
            ref[0] = dk.astype(BF16)
            ref[1] = dv.astype(BF16)

        @pl.when(live < distance)
        def _():
            ref[...] = jnp.zeros_like(ref)

    for j in range(GROUP):
        dq_ref[:, j * DH:(j + 1) * DH] = (dqt[:, j * tok:(j + 1) * tok].T * scaling).astype(BF16)


def attend(first, heads, place, at, width, mark, start, query, grad, key, value, blocks, filled):
    tok = query.shape[0]
    lead = not filled
    wide = GROUP * DH
    packed = pl.BlockSpec((2, tok, DH), lambda g: (0, 0, at + g))
    block = pl.BlockSpec((2, blocks[0].shape[1], DH), lambda g: (0, 0, place + g))
    big = pl.BlockSpec((tok, wide), lambda g: (0, first + g))
    small = pl.BlockSpec((tok, DH), lambda g: (0, first + g))
    vector = pl.BlockSpec((1, tok), lambda g: (0, 0))
    window = (REACH + 1) * tok
    lanes = GROUP * tok
    pair = (2, tok, width * DH)
    macs = heads * 5 * window * lanes * DH
    in_specs = [vector, big, big, small, small] + [block] * REACH
    out_specs = [big] + [packed] * (REACH + 1)
    out_shape = [jax.ShapeDtypeStruct(query.shape, BF16), jax.ShapeDtypeStruct(pair, F32)]
    out_shape += [jax.ShapeDtypeStruct(pair, BF16)] * REACH
    operands = [start, query, grad, key, value, *blocks]
    aliases = {}
    if lead:
        kernel = functools.partial(lead_kernel, tok)
        in_specs = [pl.BlockSpec((1, DH), lambda g: (0, 0))] + in_specs
        operands = [mark] + operands
        out_specs += [vector]
        out_shape += [jax.ShapeDtypeStruct((1, tok), jnp.int32)]
    else:
        kernel = functools.partial(follow_kernel, tok, len(filled))
        aliases = {len(operands) + n: n for n in range(len(filled))}
        in_specs += [pl.BlockSpec(memory_space=pl.ANY)] * len(filled)
        operands += filled
    return pl.pallas_call(
        kernel,
        grid=(heads,),
        in_specs=in_specs,
        out_specs=out_specs,
        scratch_shapes=[
            pltpu.VMEM((window, DH), BF16),
            pltpu.VMEM((window, DH), BF16),
            pltpu.VMEM((DH, window), BF16),
            pltpu.VMEM((DH, lanes), BF16),
            pltpu.VMEM((DH, lanes), BF16),
            pltpu.VMEM((lanes, DH), BF16),
            pltpu.VMEM((lanes, DH), BF16),
            pltpu.VMEM((window, lanes), F32),
            pltpu.VMEM((window, lanes), F32),
            pltpu.VMEM((REACH + 1, 1, lanes), F32),
            pltpu.VMEM((1, lanes), F32),
            pltpu.VMEM((1, lanes), F32),
            pltpu.VMEM((1, lanes), F32),
            pltpu.VMEM((DH, lanes), F32),
        ],
        out_shape=out_shape,
        input_output_aliases=aliases,
        compiler_params=pltpu.CompilerParams(vmem_limit_bytes=VMEM),
        cost_estimate=pl.CostEstimate(flops=COST * macs, bytes_accessed=0, transcendentals=0),
    )(*operands)


def on_device(query_in, key_in, value_in, grad_out, doc_ids):
    tok = query_in.shape[0]
    devices = lax.axis_size(AXES)
    column = lax.axis_index("inner") % ROW

    def send(block, route):
        return lax.ppermute(block, AXES, route)

    marks = (doc_ids + 1).astype(BF16)
    packs = []
    for first, heads in SENT:
        cols = slice(first * DH, (first + heads) * DH)
        pack = jnp.stack([key_in[:, cols], value_in[:, cols]])
        if first == 0:
            tail = jnp.pad(marks.reshape(-1, DH), ((0, TAIL - tok // DH), (0, 0)))
            tail = jnp.broadcast_to(jnp.tile(tail, (1, heads))[None], (2, TAIL, heads * DH))
            pack = jnp.concatenate([pack, tail], axis=1)
        packs.append(pack)

    mark = jnp.broadcast_to(marks[:1].astype(F32), (1, DH))
    start = jnp.sum((doc_ids[:, None] < doc_ids[None, :]).astype(jnp.int32), axis=0)[None]
    far = []
    operands = []
    for i, pack in enumerate(packs):
        if i > 0:
            pack, far[-1], mark, start = lax.optimization_barrier((pack, far[-1], mark, start))
        b4 = send(pack, ring(devices, REACH))
        far.append(b4)
        operands.append((jnp.where(column == ROW - 1, b4, pack), jnp.where(column < 2, pack, b4),
                         jnp.where(column == 0, pack, b4)))

    def exchange(i):
        one, two, three = operands[i]
        return (send(one, row_ring(devices, 1)), send(two, row_ring(devices, 2)),
                send(three, row_ring(devices, -1)), far[i])

    def give_back(sums):
        return send(sums[1], row_ring(devices, -1)), send(sums[2], row_ring(devices, 2)), send(sums[3], row_ring(devices, 1))

    def add_up(sums, given):
        own, d4 = sums[0], sums[4]
        g1, g2, g3 = (g.astype(F32) for g in given)
        zero = jnp.zeros((), F32)
        e4 = (d4.astype(F32) + jnp.where(column == ROW - 1, g1, zero)
              + jnp.where(column >= 1, g3, zero) + jnp.where(column >= 2, g2, zero)).astype(BF16)
        mine = (own + jnp.where(column < ROW - 1, g1, zero) + jnp.where(column == 0, g3, zero)
                + jnp.where(column < 2, g2, zero))
        return e4, mine

    blocks = [exchange(0)]
    for i in range(1, len(SENT)):
        blocks[-1], operands[i] = lax.optimization_barrier((blocks[-1], operands[i]))
        blocks.append(exchange(i))
    query_grad = None
    returned = []
    given = None
    for group in BACK:
        width = sum(CALLS[call][1] for call in group)
        at = 0
        sums = []
        for call in group:
            first, heads, sent, place = CALLS[call]
            filled = [] if query_grad is None else [query_grad, *sums]
            query_grad, *sums = attend(first, heads, place, at, width, mark, start, query_in, grad_out,
                                       key_in, value_in, blocks[sent], filled)
            if not filled:
                *sums, start = sums
            at += heads
        if given is None:
            sums[1], blocks[-1] = lax.optimization_barrier((sums[1], blocks[-1]))
        else:
            sums, given = lax.optimization_barrier((sums, given))
            returned.append(add_up(before_sums, given))
        given = give_back(sums)
        before_sums = sums

    returned.append(add_up(before_sums, given))

    results = []
    for e4, mine in returned:
        results.append((mine + send(e4, ring(devices, -REACH)).astype(F32)).astype(BF16))
    key_grad = jnp.concatenate([r[0] for r in results], axis=1)
    value_grad = jnp.concatenate([r[1] for r in results], axis=1)
    return query_grad, key_grad, value_grad


def solution(mesh):
    rows = P(AXES, None)
    return jax.shard_map(
        on_device,
        mesh=mesh,
        in_specs=(rows, rows, rows, rows, P(AXES)),
        out_specs=(rows, rows, rows),
        check_vma=False,
    )
```
